32 devices in a mesh: row: 16 (over z, y, x), col: 2 (over core).
Axes of the slice: x: 2, y: 2, z: 4, core: 2. Of those that a mesh axis runs over, the one named last changes fastest.
Arguments:
- gate_up: bfloat16 [4, 2, 14336, 4096], P(None, None, 'row', 'col'), may hold values from -0.09375 to 0.09375
- down_weight: bfloat16 [4, 4096, 14336], P(None, 'row', 'col'), may hold values from -0.046875 to 0.046875
- query_output: bfloat16 [4, 2, 4096, 4096], P(None, None, 'row', 'col'), may hold values from -0.09375 to 0.09375
- probe_gate: bfloat16 [4, 2, 16, 4096], P(None, None, None, 'col'), may hold values from -6 to 6
- probe_down: bfloat16 [4, 16, 14336], P(None, None, 'col'), may hold values from -6 to 6
- probe_query: bfloat16 [4, 2, 16, 4096], P(None, None, None, 'col'), may hold values from -6 to 6
Outputs:
- vector_gate: float32 [4, 2, 16, 4096], P(None, None, None, 'col')
- vector_down: float32 [4, 16, 14336], P(None, None, 'col')
- vector_query: float32 [4, 2, 16, 4096], P(None, None, None, 'col')
- sigma_gate: float32 [4, 2, 16], replicated
- sigma_down: float32 [4, 16], replicated
- sigma_query: float32 [4, 2, 16], replicated
The draws below stay inside these ranges and needn't reach their ends.
All inputs are finite; a program needn't handle non-finite values.
Results may differ from the reference program's by a relative error of at most 0.0033.
Values may be sent and summed in bfloat16 or wider, within the bound.
A program may use at most 128 MiB of HBM per device.

```python
import jax
import jax.numpy as jnp
from jax import lax

D = 4096
FF = 14336
LAYERS = 4
ITERS = 2
PROBES = 16


def block_scale(own_key, shape, split, least, high):
    def one(dim, parts):
        steps = jax.random.uniform(jax.random.fold_in(jax.random.fold_in(own_key, 6), dim), (parts,), jnp.float32, least / len(split), high / len(split))
        return jnp.repeat(jnp.exp(steps), shape[dim] // parts).reshape((-1,) + (1,) * (len(shape) - dim - 1))

    factor_of = one(*split[0])
    for cut in split[1:]:
        factor_of = factor_of * one(*cut)
    return factor_of


def bell_draw(rng, extent, width, bound, split=(), held_as=jnp.bfloat16):
    array = jax.random.normal(rng, extent, jnp.float32) * width
    if len(split) > 0:
        array = block_scale(rng, extent, split, -0.22, 0.18) * array
    return jnp.clip(array, min=-bound, max=bound).astype(held_as)


def setup_inputs(seed: int = 0) -> dict:
    key_list = jax.random.split(jax.random.key(seed), 7)
    gate_up = bell_draw(key_list[0], (LAYERS, 2, FF, D), D ** -0.5, 0.09375, ((2, 16), (3, 2)))
    down_weight = bell_draw(key_list[1], (LAYERS, D, FF), FF ** -0.5, 0.046875, ((1, 16), (2, 2)))
    query_output = bell_draw(key_list[2], (LAYERS, 2, D, D), D ** -0.5, 0.09375, ((2, 16), (3, 2)))
    probe_gate = bell_draw(key_list[3], (LAYERS, 2, PROBES, D), 1.0, 6.0, ((3, 2),))
    probe_down = bell_draw(key_list[4], (LAYERS, PROBES, FF), 1.0, 6.0, ((2, 2),))
    probe_query = bell_draw(key_list[5], (LAYERS, 2, PROBES, D), 1.0, 6.0, ((3, 2),))
    return dict(gate_up=gate_up, down_weight=down_weight, query_output=query_output, probe_gate=probe_gate, probe_down=probe_down, probe_query=probe_query)


epsilon = 1e-06

def power_iterate(weight, probe):
    vector = probe
    right_vec = None
    right_total = None
    for turn in range(ITERS):
        left_raw = jnp.dot(vector, weight.T, preferred_element_type=jnp.float32)
        left_mean = lax.optimization_barrier(jnp.sum(left_raw * left_raw, axis=1, keepdims=True)) / weight.shape[0]
        left_vec = left_raw.astype(jnp.bfloat16)
        right_raw = jnp.dot(left_vec, weight, preferred_element_type=jnp.float32) * lax.rsqrt(left_mean + epsilon)
        right_total = lax.optimization_barrier(jnp.sum(right_raw * right_raw, axis=1, keepdims=True))
        right_vec = right_raw * lax.rsqrt(right_total / weight.shape[1] + epsilon)
        vector = right_vec.astype(jnp.bfloat16)
    spectral = jnp.sqrt(right_total[:, 0] / weight.shape[0])
    return (right_vec, spectral)

def reference(gate_up, down_weight, query_output, probe_gate, probe_down, probe_query):
    gate_vecs, gate_sig, down_vecs, down_sig, query_vecs, query_sig = ([], [], [], [], [], [])
    for layer in range(LAYERS):
        inner_v, inner_s = ([], [])
        for which in range(2):
            result_v, result_s = power_iterate(gate_up[layer, which], probe_gate[layer, which])
            inner_v.append(result_v)
            inner_s.append(result_s)
        gate_vecs.append(jnp.stack(inner_v))
        gate_sig.append(jnp.stack(inner_s))
        result_v, result_s = power_iterate(down_weight[layer], probe_down[layer])
        down_vecs.append(result_v)
        down_sig.append(result_s)
        inner_v, inner_s = ([], [])
        for which in range(2):
            result_v, result_s = power_iterate(query_output[layer, which], probe_query[layer, which])
            inner_v.append(result_v)
            inner_s.append(result_s)
        query_vecs.append(jnp.stack(inner_v))
        query_sig.append(jnp.stack(inner_s))
    return (jnp.stack(gate_vecs), jnp.stack(down_vecs), jnp.stack(query_vecs), jnp.stack(gate_sig), jnp.stack(down_sig), jnp.stack(query_sig))
```

```python
import functools
import math

import jax
import jax.numpy as jnp
from jax import lax
from jax.experimental import pallas as pl
from jax.experimental.pallas import tpu as pltpu
from jax.sharding import PartitionSpec as P

ITERS = 2


epsilon = 1e-06

LANES = 128
LOW = 4
LEAST = 4096
VMEM_BYTES = 64 * 2**20
MESH = pl.DeviceIdType.MESH


def batch_of(count, width, rows):
    for size in range(1, count + 1):
        total = size * width
        if count % size or total < LEAST or total % (rows * LANES):
            continue
        piece = total // rows
        if width % piece == 0 and rows % size == 0:
            return size
    return None


class Group:
    def __init__(self, count, out, width, probes, rows, first):
        self.count, self.out, self.width, self.first = count, out, width, first
        self.size = batch_of(count, width, rows)
        self.batches = count // self.size
        self.piece = self.size * width // rows
        self.per = rows // self.size


def kernel(sizes, rows, probes, *refs):
    low_n, high_n = LOW, rows // LOW
    kinds = len(sizes)
    refs = list(refs)

    def take(n):
        out = refs[:n]
        del refs[:n]
        return out

    w_hbm, p_hbm, v_out = take(kinds), take(kinds), take(kinds)
    scale_out, sigma_out = take(2)
    (ws, vs, rss, prs, lss, lrs, css, crs) = (take(kinds) for _ in range(8))
    wsem, vsem, csem, rsem = (take(kinds) for _ in range(4))
    psend, precv, lsend, lrecv = (take(kinds) for _ in range(4))
    qsend, qrecv, tsend, trecv = (take(kinds) for _ in range(4))
    ltp, ltl, rtc, scale_ref, left_ref, ltsem, llsem, rtsem = take(8)

    row, col = lax.axis_index("row"), lax.axis_index("col")
    low, high = lax.rem(row, low_n), row // low_n
    plane = [lax.rem(low + k, low_n) for k in range(1, low_n)]
    line = [lax.rem(high + k, high_n) for k in range(1, high_n)]

    def at_plane(q):
        return (high * low_n + q, col)

    def at_line(h):
        return (h * low_n + low, col)

    across = (row, 1 - col)

    def remote(src, dst, send, recv, device):
        return pltpu.make_async_remote_copy(
            src_ref=src, dst_ref=dst, send_sem=send, recv_sem=recv,
            device_id=device, device_id_type=MESH)

    lane = lax.broadcasted_iota(jnp.int32, (probes, LANES), 1)

    def load_w(g, m):
        return pltpu.make_async_copy(w_hbm[g].at[m], ws[g].at[m], wsem[g].at[m])

    order = [(g, b) for g in reversed(range(kinds)) for b in range(sizes[g].batches)]

    for g, b in order:
        s = sizes[g]

        @pl.loop(0, s.size)
        def _(i, g=g, b=b, s=s):
            m = b * s.size + i
            for j in range(s.per):
                pltpu.make_async_copy(
                    p_hbm[g].at[m, :, pl.ds(j * s.piece, s.piece)],
                    vs[g].at[b, i * s.per + j], vsem[g].at[b]).start()
            load_w(g, m).start()

    barrier = pltpu.get_barrier_semaphore()
    peers = [across] + [at_plane(q) for q in plane] + [at_line(h) for h in line]
    for peer in peers:
        pl.semaphore_signal(barrier, inc=1, device_id=peer, device_id_type=MESH)
    pl.semaphore_wait(barrier, len(peers))

    scale_ref[...] = jnp.ones_like(scale_ref)

    def pick(array, m):
        return jnp.sum(jnp.where(lane == m, array, 0.0), axis=1, keepdims=True)

    def cross(g, m):
        return remote(css[g].at[m], crs[g].at[m], csem[g].at[m], rsem[g].at[m], across)

    def stage_left(turn, g, b):
        s = sizes[g]

        @pl.when(turn == 0)
        def _():
            pltpu.make_async_copy(vs[g].at[b], vs[g].at[b], vsem[g].at[b]).wait()

        @pl.loop(0, s.size)
        def _(i):
            m = b * s.size + i

            @pl.when(turn == 0)
            def _():
                load_w(g, m).wait()

            total = None
            for j in range(s.per):
                term = lax.dot_general(
                    vs[g][b, i * s.per + j],
                    ws[g][m, :, pl.ds(j * s.piece, s.piece)],
                    (((1,), (1,)), ((), ())), preferred_element_type=jnp.float32)
                total = term if total is None else total + term
            css[g][m] = total
            cross(g, m).start()

    def plane_copy(g, b, k):
        q = plane[k]
        return remote(rss[g].at[b, pl.ds(q * high_n, high_n)], prs[g].at[b, low],
                      psend[g].at[b, k], precv[g].at[b, low], at_plane(q))

    def stage_right(g, b):
        s = sizes[g]

        @pl.loop(0, s.size)
        def _(i):
            m = b * s.size + i
            cross(g, m).wait_recv()
            left = (css[g][m] + crs[g][m]) * pick(scale_ref[...], s.first + m)
            square = jnp.sum(left * left, axis=1, keepdims=True)
            left_ref[...] = jnp.where(lane == s.first + m, square, left_ref[...])
            left = left.astype(jnp.bfloat16)
            for j in range(s.per):
                rss[g][b, i * s.per + j] = jnp.dot(
                    left, ws[g][m, :, pl.ds(j * s.piece, s.piece)],
                    preferred_element_type=jnp.float32).astype(jnp.bfloat16)

        for k in range(low_n - 1):
            plane_copy(g, b, k).start()

    def line_copy(g, b, k):
        h = line[k]
        return remote(lss[g].at[b, h], lrs[g].at[b, high],
                      lsend[g].at[b, k], lrecv[g].at[b, high], at_line(h))

    def stage_plane(g, b):
        for q in plane:
            pltpu.make_async_copy(prs[g].at[b, q], prs[g].at[b, q], precv[g].at[b, q]).wait()
        for z in range(high_n):
            total = rss[g][b, low * high_n + z].astype(jnp.float32)
            for q in plane:
                total = total + prs[g][b, q, z].astype(jnp.float32)
            lss[g][b, z] = total
        for k in range(high_n - 1):
            line_copy(g, b, k).start()

    def spread_line(g, b, k):
        own = vs[g].at[b, row_piece]
        return remote(own, own, qsend[g].at[b, k], qrecv[g].at[b, high], at_line(line[k]))

    row_piece = low * high_n + high

    def stage_line(g, b):
        total = lss[g][b, high]
        for h in line:
            pltpu.make_async_copy(lrs[g].at[b, h], lrs[g].at[b, h], lrecv[g].at[b, h]).wait()
        for h in line:
            total = total + lrs[g][b, h]
        vs[g][b, row_piece] = total.astype(jnp.bfloat16)
        for k in range(high_n - 1):
            spread_line(g, b, k).start()

    def spread_plane(g, b, k):
        own = vs[g].at[b, pl.ds(low * high_n, high_n)]
        return remote(own, own, tsend[g].at[b, k], trecv[g].at[b, low], at_plane(plane[k]))

    def stage_spread(g, b):
        for h in line:
            part = vs[g].at[b, low * high_n + h]
            pltpu.make_async_copy(part, part, qrecv[g].at[b, h]).wait()
        for k in range(low_n - 1):
            spread_plane(g, b, k).start()

    def stage_last(g, b):
        s = sizes[g]
        for q in plane:
            part = vs[g].at[b, pl.ds(q * high_n, high_n)]
            pltpu.make_async_copy(part, part, trecv[g].at[b, q]).wait()
        for i in range(s.size):
            total = None
            for j in range(s.per):
                part = vs[g][b, i * s.per + j].astype(jnp.float32)
                part = jnp.sum(part * part, axis=1, keepdims=True)
                total = part if total is None else total + part
            m = s.first + b * s.size + i
            rtc[col] = jnp.where(lane == m, total, rtc[col])

    def left_plane(k):
        return remote(ltp.at[low], ltp.at[low], ltsem.at[0, k], ltsem.at[1, low], at_plane(plane[k]))

    def left_line(k):
        return remote(ltl.at[high], ltl.at[high], llsem.at[0, k], llsem.at[1, high], at_line(line[k]))

    def right_across():
        return remote(rtc.at[col], rtc.at[col], rtsem.at[0], rtsem.at[1], across)

    def per_matrix(values):
        out = jnp.full((probes, LANES), 1.0, jnp.float32)
        for s, value in zip(sizes, values):
            out = jnp.where(lane >= s.first, jnp.float32(value), out)
        return out

    outs = per_matrix([s.out * rows for s in sizes])
    ins = per_matrix([s.width * 2 for s in sizes])

    @pl.loop(0, ITERS)
    def _(turn):
        rtc[col] = jnp.zeros((probes, LANES), jnp.float32)
        left_ref[...] = jnp.zeros_like(left_ref)
        count = len(order)
        for step in range(count + 5):
            if step < count:
                stage_left(turn, *order[step])
            if 0 <= step - 1 < count:
                stage_right(*order[step - 1])
            if step == count:
                ltp[low] = left_ref[...]
                for k in range(low_n - 1):
                    left_plane(k).start()
            if 0 <= step - 3 < count:
                stage_plane(*order[step - 3])
            if step == count + 2:
                for q in plane:
                    pltpu.make_async_copy(ltp.at[q], ltp.at[q], ltsem.at[1, q]).wait()
                total = ltp[0]
                for q in range(1, low_n):
                    total = total + ltp[q]
                ltl[high] = total
                for k in range(high_n - 1):
                    left_line(k).start()
            if 0 <= step - 4 < count:
                stage_line(*order[step - 4])
            if 0 <= step - 5 < count:
                stage_spread(*order[step - 5])
        for g, b in order:
            stage_last(g, b)
        right_across().start()
        for h in line:
            pltpu.make_async_copy(ltl.at[h], ltl.at[h], llsem.at[1, h]).wait()
        total = ltl[0]
        for h in range(1, high_n):
            total = total + ltl[h]
        factor = lax.rsqrt(total / outs + epsilon)
        right_across().wait_send()
        other = rtc.at[1 - col]
        pltpu.make_async_copy(other, other, rtsem.at[1]).wait()
        right_total = (rtc[0] + rtc[1]) * factor * factor
        scale_ref[...] = factor * lax.rsqrt(right_total / ins + epsilon)
        sigma_out[...] = jnp.sqrt(right_total / outs)
        for k in range(low_n - 1):
            left_plane(k).wait_send()
        for k in range(high_n - 1):
            left_line(k).wait_send()
        for g, b in order:
            s = sizes[g]
            for i in range(s.size):
                cross(g, b * s.size + i).wait_send()
            for k in range(low_n - 1):
                plane_copy(g, b, k).wait_send()
                spread_plane(g, b, k).wait_send()
            for k in range(high_n - 1):
                line_copy(g, b, k).wait_send()
                spread_line(g, b, k).wait_send()

    scale_out[...] = scale_ref[...]
    for g in range(kinds):
        pltpu.make_async_copy(vs[g], v_out[g], vsem[g].at[0]).start()
    for g in range(kinds):
        pltpu.make_async_copy(vs[g], v_out[g], vsem[g].at[0]).wait()


def fused(gate_up, down_weight, query_output, probe_gate, probe_down, probe_query):
    rows = lax.axis_size("row")
    high_n = rows // LOW
    weights = [w.reshape((-1,) + w.shape[-2:]) for w in (gate_up, down_weight, query_output)]
    starts = [p.reshape((-1,) + p.shape[-2:]) for p in (probe_gate, probe_down, probe_query)]
    probes = starts[0].shape[1]
    sizes, first = [], 0
    for w in weights:
        sizes.append(Group(w.shape[0], w.shape[1], w.shape[2], probes, rows, first))
        first += w.shape[0]

    def each(make):
        return [make(s) for s in sizes]

    def vmem(dtype, shape_of):
        return each(lambda s: pltpu.VMEM(shape_of(s), dtype))

    def sems(shape_of):
        return each(lambda s: pltpu.SemaphoreType.DMA(shape_of(s)))

    bf, f32 = jnp.bfloat16, jnp.float32
    scratch = (
        vmem(bf, lambda s: (s.count, s.out, s.width))
        + vmem(bf, lambda s: (s.batches, rows, probes, s.piece))
        + vmem(bf, lambda s: (s.batches, rows, probes, s.piece))
        + vmem(bf, lambda s: (s.batches, LOW, high_n, probes, s.piece))
        + vmem(f32, lambda s: (s.batches, high_n, probes, s.piece))
        + vmem(f32, lambda s: (s.batches, high_n, probes, s.piece))
        + vmem(f32, lambda s: (s.count, probes, s.out))
        + vmem(f32, lambda s: (s.count, probes, s.out))
        + sems(lambda s: (s.count,))
        + sems(lambda s: (s.batches,))
        + sems(lambda s: (s.count,))
        + sems(lambda s: (s.count,))
    )
    for _ in range(2):
        for n in (LOW, LOW, high_n, high_n) if _ == 0 else (high_n, high_n, LOW, LOW):
            scratch += sems(lambda s: (s.batches, n))
    small = (probes, LANES)
    scratch += [
        pltpu.VMEM((LOW,) + small, f32),
        pltpu.VMEM((high_n,) + small, f32),
        pltpu.VMEM((2,) + small, f32),
        pltpu.VMEM(small, f32),
        pltpu.VMEM(small, f32),
        pltpu.SemaphoreType.DMA((2, LOW)),
        pltpu.SemaphoreType.DMA((2, high_n)),
        pltpu.SemaphoreType.DMA((2,)),
    ]
    work = sum(math.prod(w.shape) for w in weights)
    *vectors, scale, sigma = pl.pallas_call(
        functools.partial(kernel, sizes, rows, probes),
        out_shape=each(lambda s: jax.ShapeDtypeStruct((s.batches, rows, probes, s.piece), bf))
        + [jax.ShapeDtypeStruct(small, f32)] * 2,
        in_specs=[pl.BlockSpec(memory_space=pl.ANY)] * 6,
        out_specs=[pl.BlockSpec(memory_space=pl.ANY)] * 3
        + [pl.BlockSpec(memory_space=pltpu.VMEM)] * 2,
        scratch_shapes=scratch,
        cost_estimate=pl.CostEstimate(
            flops=4 * ITERS * probes * work, bytes_accessed=2 * work, transcendentals=0),
        compiler_params=pltpu.CompilerParams(
            collective_id=0, has_side_effects=True, vmem_limit_bytes=VMEM_BYTES),
    )(*weights, *starts)
    outs, sigmas = [], []
    for s, vector, start in zip(sizes, vectors, (probe_gate, probe_down, probe_query)):
        mine = scale[:, s.first : s.first + s.count].T
        value = vector.reshape(s.count, s.per, probes, s.piece).astype(f32) * mine[:, None, :, None]
        outs.append(value.transpose(0, 2, 1, 3).reshape(start.shape))
        sigmas.append(sigma[:, s.first : s.first + s.count].T.reshape(start.shape[:-1]))
    return (*outs, *sigmas)


def fits(*arrays):
    rows, cols = lax.axis_size("row"), lax.axis_size("col")
    weights = arrays[: len(arrays) // 2]
    held = sum(2 * math.prod(w.shape) for w in weights)
    even = all(batch_of(math.prod(w.shape[:-2]), w.shape[-1], rows) for w in weights)
    return cols == 2 and rows % LOW == 0 and even and held < 0.8 * VMEM_BYTES


def plain(gate_up, down_weight, query_output, probe_gate, probe_down, probe_query):
    row_count = lax.axis_size("row")
    col_count = lax.axis_size("col")
    weights = (gate_up, down_weight[:, None], query_output)
    vectors = (probe_gate, probe_down[:, None], probe_query)
    scaled_right = vectors
    spectral = None

    def left_factor(total, weight):
        return lax.rsqrt(total[..., None] / (weight.shape[2] * row_count) + epsilon)

    for turn in range(ITERS):
        partial_value = tuple(
            (
                jnp.einsum("lmoi,lmki->lmko", weight, vector, preferred_element_type=jnp.float32)
                for weight, vector in zip(weights, vectors)
            )
        )
        summed = lax.psum(partial_value, "col")
        squares = tuple((jnp.sum(piece * piece, axis=3) for piece in summed))
        totals = lax.psum(squares, "row")
        left_vecs = tuple((piece.astype(jnp.bfloat16) for piece in summed))
        right_partial = tuple(
            (
                jnp.einsum("lmoi,lmko->lmki", weight, left, preferred_element_type=jnp.float32)
                for weight, left in zip(weights, left_vecs)
            )
        )
        raw_sums = lax.psum(right_partial, "row")
        right_sums = tuple(
            (
                raw * left_factor(total, weight)
                for raw, total, weight in zip(raw_sums, totals, weights)
            )
        )
        right_squares = tuple((jnp.sum(piece * piece, axis=3) for piece in right_sums))
        right_totals = lax.psum(right_squares, "col")
        scaled_right = tuple(
            (
                piece * lax.rsqrt(total[..., None] / (piece.shape[3] * col_count) + epsilon)
                for piece, total in zip(right_sums, right_totals)
            )
        )
        spectral = tuple(
            (
                jnp.sqrt(total / (weight.shape[2] * row_count))
                for weight, total in zip(weights, right_totals)
            )
        )
        vectors = tuple((piece.astype(jnp.bfloat16) for piece in scaled_right))
    return (
        scaled_right[0],
        scaled_right[1][:, 0],
        scaled_right[2],
        spectral[0],
        spectral[1][:, 0],
        spectral[2],
    )


def body(*arrays):
    return (fused if fits(*arrays) else plain)(*arrays)


def solution(mesh):
    return jax.shard_map(
        body,
        mesh=mesh,
        in_specs=(
            P(None, None, "row", "col"),
            P(None, "row", "col"),
            P(None, None, "row", "col"),
            P(None, None, None, "col"),
            P(None, None, "col"),
            P(None, None, None, "col"),
        ),
        out_specs=(
            P(None, None, None, "col"),
            P(None, None, "col"),
            P(None, None, None, "col"),
            P(),
            P(),
            P(),
        ),
        check_vma=False,
    )
```

```python
import functools
import math

import jax
import jax.numpy as jnp
from jax import lax
from jax.experimental import pallas as pl
from jax.experimental.pallas import tpu as pltpu
from jax.sharding import PartitionSpec as P

ITERS = 2


epsilon = 1e-06

LANES = 128
LOW = 4
LEAST = 4096
VMEM_BYTES = 64 * 2**20
MESH = pl.DeviceIdType.MESH


def batch_of(count, width, rows):
    for size in range(1, count + 1):
        total = size * width
        if count % size or total < LEAST or total % (rows * LANES):
            continue
        piece = total // rows
        if width % piece == 0 and rows % size == 0:
            return size
    return None


class Group:
    def __init__(self, count, out, width, probes, rows, first):
        self.count, self.out, self.width, self.first = count, out, width, first
        self.size = batch_of(count, width, rows)
        self.batches = count // self.size
        self.piece = self.size * width // rows
        self.per = rows // self.size


def kernel(sizes, rows, probes, *refs):
    low_n, high_n = LOW, rows // LOW
    kinds = len(sizes)
    refs = list(refs)

    def take(n):
        out = refs[:n]
        del refs[:n]
        return out

    w_hbm, p_hbm, v_out = take(kinds), take(kinds), take(kinds)
    scale_out, sigma_out = take(2)
    (ws, vs, rss, prs, lss, lrs, css, crs) = (take(kinds) for _ in range(8))
    wsem, vsem, csem, rsem = (take(kinds) for _ in range(4))
    psend, precv, lsend, lrecv = (take(kinds) for _ in range(4))
    qsend, qrecv, tsend, trecv = (take(kinds) for _ in range(4))
    ltp, ltl, rtc, scale_ref, left_ref, ltsem, llsem, rtsem = take(8)

    row, col = lax.axis_index("row"), lax.axis_index("col")
    low, high = lax.rem(row, low_n), row // low_n
    plane = [lax.rem(low + k, low_n) for k in range(1, low_n)]
    line = [lax.rem(high + k, high_n) for k in range(1, high_n)]

    def at_plane(q):
        return (high * low_n + q, col)

    def at_line(h):
        return (h * low_n + low, col)

    across = (row, 1 - col)

    def remote(src, dst, send, recv, device):
        return pltpu.make_async_remote_copy(
            src_ref=src, dst_ref=dst, send_sem=send, recv_sem=recv,
            device_id=device, device_id_type=MESH)

    lane = lax.broadcasted_iota(jnp.int32, (probes, LANES), 1)

    def load_w(g, m):
        return pltpu.make_async_copy(w_hbm[g].at[m], ws[g].at[m], wsem[g].at[m])

    order = [(g, b) for g in reversed(range(kinds)) for b in range(sizes[g].batches)]

    for g, b in order:
        s = sizes[g]

        @pl.loop(0, s.size)
        def _(i, g=g, b=b, s=s):
            m = b * s.size + i
            for j in range(s.per):
                pltpu.make_async_copy(
                    p_hbm[g].at[m, :, pl.ds(j * s.piece, s.piece)],
                    vs[g].at[b, i * s.per + j], vsem[g].at[b]).start()
            load_w(g, m).start()

    barrier = pltpu.get_barrier_semaphore()
    peers = [across] + [at_plane(q) for q in plane] + [at_line(h) for h in line]
    for peer in peers:
        pl.semaphore_signal(barrier, inc=1, device_id=peer, device_id_type=MESH)
    pl.semaphore_wait(barrier, len(peers))

    scale_ref[...] = jnp.ones_like(scale_ref)

    def pick(array, m):
        return jnp.sum(jnp.where(lane == m, array, 0.0), axis=1, keepdims=True)

    def cross(g, m):
        return remote(css[g].at[m], crs[g].at[m], csem[g].at[m], rsem[g].at[m], across)

    def stage_left(turn, g, b):
        s = sizes[g]

        @pl.when(turn == 0)
        def _():
            pltpu.make_async_copy(vs[g].at[b], vs[g].at[b], vsem[g].at[b]).wait()

        @pl.loop(0, s.size)
        def _(i):
            m = b * s.size + i

            @pl.when(turn == 0)
            def _():
                load_w(g, m).wait()

            total = None
            for j in range(s.per):
                term = lax.dot_general(
                    vs[g][b, i * s.per + j],
                    ws[g][m, :, pl.ds(j * s.piece, s.piece)],
                    (((1,), (1,)), ((), ())), preferred_element_type=jnp.float32)
                total = term if total is None else total + term
            css[g][m] = total
            cross(g, m).start()

    def plane_copy(g, b, k):
        q = plane[k]
        return remote(rss[g].at[b, pl.ds(q * high_n, high_n)], prs[g].at[b, low],
                      psend[g].at[b, k], precv[g].at[b, low], at_plane(q))

    def stage_right(g, b):
        s = sizes[g]

        @pl.loop(0, s.size)
        def _(i):
            m = b * s.size + i
            cross(g, m).wait_recv()
            left = (css[g][m] + crs[g][m]) * pick(scale_ref[...], s.first + m)
            square = jnp.sum(left * left, axis=1, keepdims=True)
            left_ref[...] = jnp.where(lane == s.first + m, square, left_ref[...])
            left = left.astype(jnp.bfloat16)
            for j in range(s.per):
                rss[g][b, i * s.per + j] = jnp.dot(
                    left, ws[g][m, :, pl.ds(j * s.piece, s.piece)],
                    preferred_element_type=jnp.float32).astype(jnp.bfloat16)

        for k in range(low_n - 1):
            plane_copy(g, b, k).start()

    def line_copy(g, b, k):
        h = line[k]
        return remote(lss[g].at[b, h], lrs[g].at[b, high],
                      lsend[g].at[b, k], lrecv[g].at[b, high], at_line(h))

    def stage_plane(g, b):
        for q in plane:
            pltpu.make_async_copy(prs[g].at[b, q], prs[g].at[b, q], precv[g].at[b, q]).wait()
        for z in range(high_n):
            total = rss[g][b, low * high_n + z].astype(jnp.float32)
            for q in plane:
                total = total + prs[g][b, q, z].astype(jnp.float32)
            lss[g][b, z] = total
        for k in range(high_n - 1):
            line_copy(g, b, k).start()

    def spread_line(g, b, k):
        own = vs[g].at[b, row_piece]
        return remote(own, own, qsend[g].at[b, k], qrecv[g].at[b, high], at_line(line[k]))

    row_piece = low * high_n + high

    def stage_line(g, b):
        total = lss[g][b, high]
        for h in line:
            pltpu.make_async_copy(lrs[g].at[b, h], lrs[g].at[b, h], lrecv[g].at[b, h]).wait()
        for h in line:
            total = total + lrs[g][b, h]
        vs[g][b, row_piece] = total.astype(jnp.bfloat16)
        for k in range(high_n - 1):
            spread_line(g, b, k).start()

    def spread_plane(g, b, k):
        own = vs[g].at[b, pl.ds(low * high_n, high_n)]
        return remote(own, own, tsend[g].at[b, k], trecv[g].at[b, low], at_plane(plane[k]))

    def stage_spread(g, b):
        for h in line:
            part = vs[g].at[b, low * high_n + h]
            pltpu.make_async_copy(part, part, qrecv[g].at[b, h]).wait()
        for k in range(low_n - 1):
            spread_plane(g, b, k).start()

    def stage_last(g, b):
        s = sizes[g]
        for q in plane:
            part = vs[g].at[b, pl.ds(q * high_n, high_n)]
            pltpu.make_async_copy(part, part, trecv[g].at[b, q]).wait()
        for i in range(s.size):
            total = None
            for j in range(s.per):
                part = vs[g][b, i * s.per + j].astype(jnp.float32)
                part = jnp.sum(part * part, axis=1, keepdims=True)
                total = part if total is None else total + part
            m = s.first + b * s.size + i
            rtc[col] = jnp.where(lane == m, total, rtc[col])

    def left_plane(k):
        return remote(ltp.at[low], ltp.at[low], ltsem.at[0, k], ltsem.at[1, low], at_plane(plane[k]))

    def left_line(k):
        return remote(ltl.at[high], ltl.at[high], llsem.at[0, k], llsem.at[1, high], at_line(line[k]))

    def right_across():
        return remote(rtc.at[col], rtc.at[col], rtsem.at[0], rtsem.at[1], across)

    def per_matrix(values):
        out = jnp.full((probes, LANES), 1.0, jnp.float32)
        for s, value in zip(sizes, values):
            out = jnp.where(lane >= s.first, jnp.float32(value), out)
        return out

    outs = per_matrix([s.out * rows for s in sizes])
    ins = per_matrix([s.width * 2 for s in sizes])

    @pl.loop(0, ITERS)
    def _(turn):
        rtc[col] = jnp.zeros((probes, LANES), jnp.float32)
        left_ref[...] = jnp.zeros_like(left_ref)
        count = len(order)
        for step in range(count + 7):
            if step < count:
                stage_left(turn, *order[step])
            if 0 <= step - 1 < count:
                stage_right(*order[step - 1])
            if step == count:
                ltp[low] = left_ref[...]
                for k in range(low_n - 1):
                    left_plane(k).start()
            if 0 <= step - 3 < count:
                stage_plane(*order[step - 3])
            if step == count + 3:
                for q in plane:
                    pltpu.make_async_copy(ltp.at[q], ltp.at[q], ltsem.at[1, q]).wait()
                total = ltp[0]
                for q in range(1, low_n):
                    total = total + ltp[q]
                ltl[high] = total
                for k in range(high_n - 1):
                    left_line(k).start()
            if 0 <= step - 5 < count:
                stage_line(*order[step - 5])
            if 0 <= step - 7 < count:
                stage_spread(*order[step - 7])
        for g, b in order:
            stage_last(g, b)
        right_across().start()
        for h in line:
            pltpu.make_async_copy(ltl.at[h], ltl.at[h], llsem.at[1, h]).wait()
        total = ltl[0]
        for h in range(1, high_n):
            total = total + ltl[h]
        factor = lax.rsqrt(total / outs + epsilon)
        right_across().wait_send()
        other = rtc.at[1 - col]
        pltpu.make_async_copy(other, other, rtsem.at[1]).wait()
        right_total = (rtc[0] + rtc[1]) * factor * factor
        scale_ref[...] = factor * lax.rsqrt(right_total / ins + epsilon)
        sigma_out[...] = jnp.sqrt(right_total / outs)
        for k in range(low_n - 1):
            left_plane(k).wait_send()
        for k in range(high_n - 1):
            left_line(k).wait_send()
        for g, b in order:
            s = sizes[g]
            for i in range(s.size):
                cross(g, b * s.size + i).wait_send()
            for k in range(low_n - 1):
                plane_copy(g, b, k).wait_send()
                spread_plane(g, b, k).wait_send()
            for k in range(high_n - 1):
                line_copy(g, b, k).wait_send()
                spread_line(g, b, k).wait_send()

    scale_out[...] = scale_ref[...]
    for g in range(kinds):
        pltpu.make_async_copy(vs[g], v_out[g], vsem[g].at[0]).start()
    for g in range(kinds):
        pltpu.make_async_copy(vs[g], v_out[g], vsem[g].at[0]).wait()


def fused(gate_up, down_weight, query_output, probe_gate, probe_down, probe_query):
    rows = lax.axis_size("row")
    high_n = rows // LOW
    weights = [w.reshape((-1,) + w.shape[-2:]) for w in (gate_up, down_weight, query_output)]
    starts = [p.reshape((-1,) + p.shape[-2:]) for p in (probe_gate, probe_down, probe_query)]
    probes = starts[0].shape[1]
    sizes, first = [], 0
    for w in weights:
        sizes.append(Group(w.shape[0], w.shape[1], w.shape[2], probes, rows, first))
        first += w.shape[0]

    def each(make):
        return [make(s) for s in sizes]

    def vmem(dtype, shape_of):
        return each(lambda s: pltpu.VMEM(shape_of(s), dtype))

    def sems(shape_of):
        return each(lambda s: pltpu.SemaphoreType.DMA(shape_of(s)))

    bf, f32 = jnp.bfloat16, jnp.float32
    scratch = (
        vmem(bf, lambda s: (s.count, s.out, s.width))
        + vmem(bf, lambda s: (s.batches, rows, probes, s.piece))
        + vmem(bf, lambda s: (s.batches, rows, probes, s.piece))
        + vmem(bf, lambda s: (s.batches, LOW, high_n, probes, s.piece))
        + vmem(f32, lambda s: (s.batches, high_n, probes, s.piece))
        + vmem(f32, lambda s: (s.batches, high_n, probes, s.piece))
        + vmem(f32, lambda s: (s.count, probes, s.out))
        + vmem(f32, lambda s: (s.count, probes, s.out))
        + sems(lambda s: (s.count,))
        + sems(lambda s: (s.batches,))
        + sems(lambda s: (s.count,))
        + sems(lambda s: (s.count,))
    )
    for _ in range(2):
        for n in (LOW, LOW, high_n, high_n) if _ == 0 else (high_n, high_n, LOW, LOW):
            scratch += sems(lambda s: (s.batches, n))
    small = (probes, LANES)
    scratch += [
        pltpu.VMEM((LOW,) + small, f32),
        pltpu.VMEM((high_n,) + small, f32),
        pltpu.VMEM((2,) + small, f32),
        pltpu.VMEM(small, f32),
        pltpu.VMEM(small, f32),
        pltpu.SemaphoreType.DMA((2, LOW)),
        pltpu.SemaphoreType.DMA((2, high_n)),
        pltpu.SemaphoreType.DMA((2,)),
    ]
    work = sum(math.prod(w.shape) for w in weights)
    *vectors, scale, sigma = pl.pallas_call(
        functools.partial(kernel, sizes, rows, probes),
        out_shape=each(lambda s: jax.ShapeDtypeStruct((s.batches, rows, probes, s.piece), bf))
        + [jax.ShapeDtypeStruct(small, f32)] * 2,
        in_specs=[pl.BlockSpec(memory_space=pl.ANY)] * 6,
        out_specs=[pl.BlockSpec(memory_space=pl.ANY)] * 3
        + [pl.BlockSpec(memory_space=pltpu.VMEM)] * 2,
        scratch_shapes=scratch,
        cost_estimate=pl.CostEstimate(
            flops=4 * ITERS * probes * work, bytes_accessed=2 * work, transcendentals=0),
        compiler_params=pltpu.CompilerParams(
            collective_id=0, has_side_effects=True, vmem_limit_bytes=VMEM_BYTES),
    )(*weights, *starts)
    outs, sigmas = [], []
    for s, vector, start in zip(sizes, vectors, (probe_gate, probe_down, probe_query)):
        mine = scale[:, s.first : s.first + s.count].T
        value = vector.reshape(s.count, s.per, probes, s.piece).astype(f32) * mine[:, None, :, None]
        outs.append(value.transpose(0, 2, 1, 3).reshape(start.shape))
        sigmas.append(sigma[:, s.first : s.first + s.count].T.reshape(start.shape[:-1]))
    return (*outs, *sigmas)


def fits(*arrays):
    rows, cols = lax.axis_size("row"), lax.axis_size("col")
    weights = arrays[: len(arrays) // 2]
    held = sum(2 * math.prod(w.shape) for w in weights)
    even = all(batch_of(math.prod(w.shape[:-2]), w.shape[-1], rows) for w in weights)
    return cols == 2 and rows % LOW == 0 and even and held < 0.8 * VMEM_BYTES


def plain(gate_up, down_weight, query_output, probe_gate, probe_down, probe_query):
    row_count = lax.axis_size("row")
    col_count = lax.axis_size("col")
    weights = (gate_up, down_weight[:, None], query_output)
    vectors = (probe_gate, probe_down[:, None], probe_query)
    scaled_right = vectors
    spectral = None

    def left_factor(total, weight):
        return lax.rsqrt(total[..., None] / (weight.shape[2] * row_count) + epsilon)

    for turn in range(ITERS):
        partial_value = tuple(
            (
                jnp.einsum("lmoi,lmki->lmko", weight, vector, preferred_element_type=jnp.float32)
                for weight, vector in zip(weights, vectors)
            )
        )
        summed = lax.psum(partial_value, "col")
        squares = tuple((jnp.sum(piece * piece, axis=3) for piece in summed))
        totals = lax.psum(squares, "row")
        left_vecs = tuple((piece.astype(jnp.bfloat16) for piece in summed))
        right_partial = tuple(
            (
                jnp.einsum("lmoi,lmko->lmki", weight, left, preferred_element_type=jnp.float32)
                for weight, left in zip(weights, left_vecs)
            )
        )
        raw_sums = lax.psum(right_partial, "row")
        right_sums = tuple(
            (
                raw * left_factor(total, weight)
                for raw, total, weight in zip(raw_sums, totals, weights)
            )
        )
        right_squares = tuple((jnp.sum(piece * piece, axis=3) for piece in right_sums))
        right_totals = lax.psum(right_squares, "col")
        scaled_right = tuple(
            (
                piece * lax.rsqrt(total[..., None] / (piece.shape[3] * col_count) + epsilon)
                for piece, total in zip(right_sums, right_totals)
            )
        )
        spectral = tuple(
            (
                jnp.sqrt(total / (weight.shape[2] * row_count))
                for weight, total in zip(weights, right_totals)
            )
        )
        vectors = tuple((piece.astype(jnp.bfloat16) for piece in scaled_right))
    return (
        scaled_right[0],
        scaled_right[1][:, 0],
        scaled_right[2],
        spectral[0],
        spectral[1][:, 0],
        spectral[2],
    )


def body(*arrays):
    return (fused if fits(*arrays) else plain)(*arrays)


def solution(mesh):
    return jax.shard_map(
        body,
        mesh=mesh,
        in_specs=(
            P(None, None, "row", "col"),
            P(None, "row", "col"),
            P(None, None, "row", "col"),
            P(None, None, None, "col"),
            P(None, None, "col"),
            P(None, None, None, "col"),
        ),
        out_specs=(
            P(None, None, None, "col"),
            P(None, None, "col"),
            P(None, None, None, "col"),
            P(),
            P(),
            P(),
        ),
        check_vma=False,
    )
```
